512 devices in a mesh: grp: 8 (over y_hi, core), fsdp: 64 (over z, x, y_lo).
Axes of the slice: x: 4, y: 8 (y_hi: 4, y_lo: 2; y = y_hi * 2 + y_lo), z: 8, core: 2. Of those that a mesh axis runs over, the one named last changes fastest.
Arguments:
- hidden_in: bfloat16 [64, 8, 224, 2560], P('fsdp', 'grp'), may hold values from -16 to 16
- queries: bfloat16 [64, 8, 224, 2560], P('fsdp', 'grp'), may hold values from -5 to 5
- keys: bfloat16 [64, 8, 224, 512], P('fsdp', 'grp'), may hold values from -5 to 5
- logp_grad: bfloat16 [64, 8, 224, 2560], P('fsdp', 'grp'), may hold values from -96 to 96
- lengths: int32 [64, 8], P('fsdp', 'grp'), may hold values from 28 to 224, as said below
- rewards: int32 [64, 8], P('fsdp', 'grp'), may hold values from 0 to 3
- w_value: bfloat16 [2560, 512], P('fsdp'), may hold values from -1 to 1
Outputs:
- grad_weight: float32 [2560, 512], P('fsdp', 'grp')
- grad_input: bfloat16 [64, 8, 224, 2560], P('fsdp', 'grp')
The draws below stay inside these ranges and needn't reach their ends.
Inputs may be any that keep to these rules, and one draw needn't show every extreme that they name: `lengths`: every prompt has one response of exactly 224 tokens; the others have at least 28.
All inputs are finite; a program needn't handle non-finite values.
Results may differ from the reference program's by a relative error of at most 0.015.
Values may be sent and summed in bfloat16 or wider, within the bound.
A program may use at most 64 MiB of HBM per device.

```python
import jax
import jax.numpy as jnp
from jax import lax

DW = 2560
KV_HEADS = 4
RATIO = 5
HEAD_WIDTH = 128
LEN = 224
QW = 2560
KW = 512
PROMPTS = 64
GROUP = 8


def draw_keys(key, part):
    key = jax.random.fold_in(key, 5)
    result = jax.random.truncated_normal(key, -4.0, 4.0, (PROMPTS, GROUP, LEN, KV_HEADS * HEAD_WIDTH), jnp.float32)
    return result.astype(jnp.bfloat16)


def draw_queries(key, part):
    key = jax.random.fold_in(key, 7)
    result = jax.random.truncated_normal(key, -4.0, 4.0, (PROMPTS, GROUP, LEN, KV_HEADS * RATIO * HEAD_WIDTH), jnp.float32)
    return result.astype(jnp.bfloat16)


def draw_lengths(key, part):
    key = jax.random.fold_in(key, 11)
    others = jax.random.randint(jax.random.fold_in(key, 1), (PROMPTS, GROUP), LEN // 8, LEN + 1)
    longest = jax.random.randint(jax.random.fold_in(key, 2), (PROMPTS, 1), 0, GROUP)
    members = jnp.arange(GROUP)[None, :]
    return jnp.where(members == longest, LEN, others).astype(jnp.int32)


def touch_ends(entries, key, smallest, high):
    longest = entries.shape.index(max(entries.shape))
    spots = []
    for shift in (0, 1):
        where = [jax.random.randint(jax.random.fold_in(key, axis), (), 0, length) for axis, length in enumerate(entries.shape)]
        where[longest] = (where[longest] + shift) % entries.shape[longest]
        spots.append(tuple(where))
    return entries.at[spots[0]].set(smallest).at[spots[1]].set(high)


def strengthened(values, own_key, source, target, parts, factor):
    owner, partner = [(jnp.arange(values.shape[position]) // (values.shape[position] // parts)).reshape([-1 if axis == position else 1 for axis in range(values.ndim)]) for position in (source, target)]
    chosen = jax.random.permutation(own_key, parts)[partner]
    strong = (owner == chosen) | (owner == (partner + parts // 2) % parts)
    return jnp.where(strong, factor * values, values)


def levels(stream_key, shape, shards, low, high):
    def one(dim, blocks):
        steps = jax.random.uniform(jax.random.fold_in(jax.random.fold_in(stream_key, 6), dim), (blocks,), jnp.float32, low / len(shards), high / len(shards))
        return jnp.repeat(jnp.exp(steps), shape[dim] // blocks).reshape((-1,) + (1,) * (len(shape) - dim - 1))

    level = one(*shards[0])
    for cut in shards[1:]:
        level = level * one(*cut)
    return level


def bell_draw(rng, extent, scale, reach, split=(), dtype=jnp.bfloat16):
    entries = jax.random.normal(rng, extent, jnp.float32) * scale
    if len(split) > 0:
        entries = levels(rng, extent, split, -0.22, 0.18) * entries
    return jnp.clip(entries, min=-reach, max=reach).astype(dtype)


def gaussian_with(stream_key, shape, width, limit, pieces, heavy, kind=jnp.bfloat16):
    entries = width * jax.random.normal(stream_key, shape, jnp.float32)
    if pieces:
        entries = entries * levels(stream_key, shape, pieces, -0.22, 0.18)
    return jnp.clip(strengthened(entries, jax.random.fold_in(stream_key, 3), *heavy), -limit, limit).astype(kind)


def setup_inputs(seed: int = 0) -> dict:
    splits = jax.random.split(jax.random.key(seed), 8)
    hidden_in = gaussian_with(splits[0], (PROMPTS, GROUP, LEN, DW), 1.0, 16.0, ((0, 64), (1, 8)), (0, 3, 64, 4.0))
    queries = draw_queries(jax.random.fold_in(splits[7], 71), 0)
    keys = draw_keys(jax.random.fold_in(splits[7], 71), 0)
    logp_grad = bell_draw(splits[3], (PROMPTS, GROUP, LEN, QW), 16.0, 96.0, ((0, 64), (1, 8)))
    lengths = draw_lengths(jax.random.fold_in(splits[7], 71), 0)
    rewards = touch_ends(jax.random.randint(splits[5], (PROMPTS, GROUP), 0, 4), jax.random.fold_in(splits[5], 1), 0, 3).astype(jnp.int32)
    w_value = bell_draw(splits[6], (DW, KW), (KW // 16) ** -0.5, 1.0, ((0, 64),))
    return dict(hidden_in=hidden_in, queries=queries, keys=keys, logp_grad=logp_grad, lengths=lengths, rewards=rewards, w_value=w_value)


def value_cotangent(queries, keys, logp_grad, factor, length):
    seq_len = queries.shape[0]
    query_head_rows = queries.astype(jnp.float32).reshape(seq_len, KV_HEADS, RATIO, HEAD_WIDTH)
    key_head_rows = keys.astype(jnp.float32).reshape(seq_len, KV_HEADS, HEAD_WIDTH)
    attention_logits = jnp.einsum('wzhl,kzl->zhwk', query_head_rows, key_head_rows) * HEAD_WIDTH ** (-0.5)
    positions = jnp.arange(seq_len)
    causal = positions[:, None] >= positions[None, :]
    attention_logits = jnp.where(causal, attention_logits, -1e+30)
    shifted = jnp.exp(attention_logits - lax.optimization_barrier(jnp.max(attention_logits, axis=-1, keepdims=True)))
    attention_probability = (shifted / lax.optimization_barrier(jnp.sum(shifted, axis=-1, keepdims=True))).astype(jnp.bfloat16)
    weights = jnp.where(positions < length, factor, 0.0).astype(jnp.float32)
    scaled_scores = (logp_grad.astype(jnp.float32) * weights[:, None]).astype(jnp.bfloat16)
    scaled_scores = scaled_scores.reshape(seq_len, KV_HEADS, RATIO, HEAD_WIDTH)
    value_vectors = jnp.einsum('zibl,bziq->lzq', attention_probability.astype(jnp.float32), scaled_scores.astype(jnp.float32))
    return value_vectors.astype(jnp.bfloat16).reshape(seq_len, KV_HEADS * HEAD_WIDTH)

def reference(hidden_in, queries, keys, logp_grad, lengths, rewards, w_value):
    scores_int = rewards.astype(jnp.float32)
    average = lax.optimization_barrier(jnp.sum(scores_int, axis=1, keepdims=True)) / GROUP
    second = lax.optimization_barrier(jnp.sum(scores_int * scores_int, axis=1, keepdims=True)) / GROUP
    spread = jnp.maximum(jnp.sqrt(second - average * average), 1.0)
    advantage = (scores_int - average) / spread
    factor = -advantage / (GROUP * lengths.astype(jnp.float32))
    count_all = PROMPTS * GROUP
    flat_in = hidden_in.reshape(count_all, LEN, DW)
    flat_q = queries.reshape(count_all, LEN, QW)
    flat_k = keys.reshape(count_all, LEN, KW)
    flat_g = logp_grad.reshape(count_all, LEN, QW)
    flat_f = factor.reshape(count_all)
    flat_n = lengths.reshape(count_all)

    def step(running, items):
        inputs, query_rows, key_rows, grad_rows, weight, length = items
        value_grad = value_cotangent(query_rows, key_rows, grad_rows, weight, length)
        term = lax.dot_general(inputs, value_grad, (((0,), (0,)), ((), ())), preferred_element_type=jnp.float32)
        term = term.astype(jnp.bfloat16).astype(jnp.float32)
        result = jnp.dot(value_grad, w_value.T, preferred_element_type=jnp.float32).astype(jnp.bfloat16)
        return (running + term, result)
    start_grad = jnp.zeros((DW, KW), jnp.float32)
    summed, inputs_grad = lax.scan(step, start_grad, (flat_in, flat_q, flat_k, flat_g, flat_f, flat_n))
    return (summed, inputs_grad.reshape(PROMPTS, GROUP, LEN, DW))
```

```python
import jax
import jax.numpy as jnp
from jax import lax
from jax.experimental import pallas as pl
from jax.experimental.pallas import tpu as pltpu
from jax.sharding import PartitionSpec as P

F32 = jnp.float32
BF16 = jnp.bfloat16
MESH = pl.DeviceIdType.MESH

HEADS = 4
RATIO = 5
WIDTH = 128
LEN = 224
FEATURES = 2560
HALF = 1280
ROWS = 40
MEMBERS = 8
NX, NY, NZ = 4, 8, 8
EXPONENT_SCALE = 1.4426950408889634 * WIDTH ** -0.5
NT = (((1,), (1,)), ((), ()))


def softmax_columns(scores, weight):
    top = jnp.max(scores, axis=0, keepdims=True)
    grown = jnp.exp2((scores - top) * EXPONENT_SCALE)
    total = jnp.sum(grown, axis=0, keepdims=True)
    return (grown * (weight / total)).astype(BF16)


def head_gradient(keys, queries, cotangent, alive):
    upper = lax.broadcasted_iota(jnp.int32, (128, 128), 0) <= lax.broadcasted_iota(jnp.int32, (128, 128), 1)
    corner = lax.broadcasted_iota(jnp.int32, (96, 96), 0) <= lax.broadcasted_iota(jnp.int32, (96, 96), 1)
    total = None
    for h in range(RATIO):
        cols = slice(h * WIDTH, (h + 1) * WIDTH)
        early = lax.dot_general(keys[:128], queries[:128, cols], NT, preferred_element_type=F32)
        late = lax.dot_general(keys, queries[128:, cols], NT, preferred_element_type=F32)
        early = jnp.where(upper, early, -1e30)
        late = jnp.concatenate([late[:128], jnp.where(corner, late[128:], -1e30)], 0)
        early = softmax_columns(early, alive[:, :128])
        late = softmax_columns(late, alive[:, 128:])
        probs = jnp.concatenate(
            [jnp.concatenate([early, jnp.zeros((96, 128), BF16)], 0), late], 1
        )
        part = jnp.dot(probs, cotangent[:, cols], preferred_element_type=F32)
        total = part if total is None else total + part
    return total


def kernel(
    hid, queries, keys, logp, length_ref, reward_ref, w_ref,
    gw_ref, gi_ref,
    qb, kb, gb, hb, wb, ht, ub, vg, rw_src, rw,
    pb, s1s, s1r, qs, s2s, s2r, rs, s3s, s3r, zo, zs, zr, fs, fr,
    ws, wg, wf, go, gs,
    in_sem, ex_send, ex_recv, rw_send, rw_recv,
    s1_send, s1_recv, s2_send, s2_recv, s3_send, s3_recv, z_send, z_recv, f_send, f_recv,
    wz_send, wz_recv, wx_send, wx_recv, wy_send, wy_recv, go_sem, gs_send, gs_recv,
):
    g = lax.axis_index("grp")
    f = lax.axis_index("fsdp")
    c = lax.rem(g, 2)
    yh = g // 2
    yl = lax.rem(f, 2)
    x = lax.rem(f // 2, NX)
    z = f // (2 * NX)
    zc = z // 4
    zi = lax.rem(z, 4)
    y = 2 * yh + yl

    def at(z_, x_, y_, c_):
        return (2 * (y_ // 2) + c_, (z_ * NX + x_) * 2 + lax.rem(y_, 2))

    sibling = at(z, x, y, 1 - c)
    group = [(lax.rem(g + d, MEMBERS), f) for d in range(1, MEMBERS)]
    up = at(z, x, lax.rem(y + 1, NY), c)
    down = at(z, x, lax.rem(y + NY - 1, NY), c)
    xs = [at(z, lax.rem(x + d, NX), y, c) for d in range(1, NX)]
    zs_both = [at(lax.rem(z + d, NZ), x, y, k) for d in range(1, NZ) for k in range(2)]

    barrier = pltpu.get_barrier_semaphore()
    partners = group + [up, down] + xs + zs_both
    for device in partners:
        pl.semaphore_signal(barrier, inc=1, device_id=device, device_id_type=MESH)

    def remote(src, dst, send, recv, device):
        return pltpu.make_async_remote_copy(
            src_ref=src, dst_ref=dst, send_sem=send, recv_sem=recv, device_id=device, device_id_type=MESH
        )

    loads = []
    for j in range(HEADS):
        wide = pl.ds(j * RATIO * WIDTH, RATIO * WIDTH)
        loads.append([
            pltpu.make_async_copy(keys.at[:, pl.ds(j * WIDTH, WIDTH)], kb.at[j], in_sem.at[3 * j]),
            pltpu.make_async_copy(queries.at[:, wide], qb.at[j], in_sem.at[3 * j + 1]),
            pltpu.make_async_copy(logp.at[:, wide], gb.at[j], in_sem.at[3 * j + 2]),
        ])
    load_w = pltpu.make_async_copy(w_ref, wb, in_sem.at[12])
    load_h = pltpu.make_async_copy(hid.at[:, pl.ds(pl.multiple_of(c * HALF, 128), HALF)], hb.at[0], in_sem.at[13])
    for copy in loads[0] + loads[1] + [load_w] + loads[2] + loads[3] + [load_h]:
        copy.start()

    reward = reward_ref[0, 0].astype(F32)
    length = length_ref[0, 0]
    row = lax.broadcasted_iota(jnp.int32, (8, 128), 0)
    rw_src[...] = jnp.where(row == 0, reward, length.astype(F32))

    alive = jnp.where(lax.broadcasted_iota(jnp.int32, (1, LEN), 1) < length, 1.0, 0.0).astype(F32)
    for j in range(HEADS):
        for copy in loads[j]:
            copy.wait()
        ub[0, j] = head_gradient(kb[j], qb[j], gb[j], alive).astype(BF16)

    load_w.wait()
    shard = wb[...].astype(F32)
    ws[...] = jnp.concatenate([shard[:, p * 128:(p + 1) * 128] for p in range(4)], 0).astype(BF16)

    @pl.when(c == zc)
    def _():
        wg[yl, x, zi] = ws[...]

    load_h.wait()
    for b in range(10):
        cols = slice(b * 128, (b + 1) * 128)
        ht[0, cols, :] = hb[0, :, cols].T

    pl.semaphore_wait(barrier, len(partners))

    reward_copies = [remote(rw_src, rw.at[d], rw_send.at[d], rw_recv.at[d], group[d - 1]) for d in range(1, MEMBERS)]
    for copy in reward_copies:
        copy.start()
    share_u = remote(ub.at[0], ub.at[1], ex_send.at[0], ex_recv.at[0], sibling)
    share_h = remote(
        hid.at[:, pl.ds(pl.multiple_of((1 - c) * HALF, 128), HALF)], hb.at[1], ex_send.at[1], ex_recv.at[1], sibling
    )
    share_h.start()
    share_u.start()

    def w_send(i):
        other = 4 * c + i
        return remote(ws, wg.at[yl, x, zi], wz_send.at[i], wz_recv.at[zi], at(other, x, y, zc))

    def w_arrival(i):
        return remote(ws, wg.at[yl, x, i], wz_send.at[i], wz_recv.at[i], at(4 * c + i, x, y, zc))

    for i in range(4):
        @pl.when(4 * c + i != z)
        def _(i=i):
            w_send(i).start()

    share_h.wait_recv()
    for b in range(10):
        cols = slice(b * 128, (b + 1) * 128)
        ht[1, cols, :] = hb[1, :, cols].T
    share_u.wait_recv()

    for copy in reward_copies:
        copy.wait_recv()
    rw[0] = rw_src[...]
    everyone = rw[...]
    rewards = everyone[:, 0:1, :]
    average = jnp.sum(rewards, axis=0) / MEMBERS
    second = jnp.sum(rewards * rewards, axis=0) / MEMBERS
    spread = jnp.maximum(jnp.sqrt(second - average * average), 1.0)

    def factor_of(rows):
        return -((rows[0:1] - average) / spread) / (MEMBERS * rows[1:2])

    own_factor = factor_of(rw_src[...])
    other_factor = factor_of(rw[7 - 6 * c])

    s1 = []
    for j in range(HEADS):
        lanes = slice(j * 128, (j + 1) * 128)
        vg[0, :, lanes] = (ub[0, j].astype(F32) * own_factor).astype(BF16)
        vg[1, :, lanes] = (ub[1, j].astype(F32) * other_factor).astype(BF16)
        for b in range(4):
            rows = slice(b * 320, (b + 1) * 320)
            part = jnp.dot(ht[0, rows, :], vg[0, :, lanes], preferred_element_type=F32)
            part += jnp.dot(ht[1, rows, :], vg[1, :, lanes], preferred_element_type=F32)
            pb[j, b * 4:(b + 1) * 4] = part.reshape(4, 2, ROWS, 128)
        s1s[j] = pb[j, :, 1 - yl].reshape(640, 128).astype(BF16)
        copies = [
            remote(s1s.at[j, pl.ds(0, 320)], s1r.at[j, pl.ds(0, 320)], s1_send.at[j, 0], s1_recv.at[j, 0], up),
            remote(s1s.at[j, pl.ds(320, 320)], s1r.at[j, pl.ds(320, 320)], s1_send.at[j, 1], s1_recv.at[j, 1], down),
        ]
        for copy in copies:
            copy.start()
        s1.append(copies)

    for i in range(4):
        @pl.when(4 * c + i != z)
        def _(i=i):
            w_arrival(i).wait_recv()
    wx = [remote(wg.at[yl, x], wg.at[yl, x], wx_send.at[d], wx_recv.at[d], xs[d]) for d in range(NX - 1)]
    for copy in wx:
        copy.start()

    s2 = []
    for j in range(HEADS):
        for copy in s1[j]:
            copy.wait_recv()
        qs[j] = (pb[j, :, yl] + s1r[j].astype(F32).reshape(16, ROWS, 128)).reshape(4, 4, ROWS, 128)
        copies = []
        for d in range(NX - 1):
            s2s[j, d] = qs[j, :, lax.rem(x + d + 1, NX)].reshape(160, 128).astype(BF16)
            copies.append(remote(s2s.at[j, d], s2r.at[j, d], s2_send.at[j, d], s2_recv.at[j, d], xs[d]))
            copies[-1].start()
        s2.append(copies)

    def wx_arrival(d):
        return remote(
            wg.at[yl, x], wg.at[yl, lax.rem(x + NX - 1 - d, NX)], wx_send.at[d], wx_recv.at[d], xs[d]
        )

    for d in range(NX - 1):
        wx_arrival(d).wait_recv()
    wy = [
        remote(wg.at[yl, pl.ds(0, 2)], wg.at[yl, pl.ds(0, 2)], wy_send.at[0], wy_recv.at[0], up),
        remote(wg.at[yl, pl.ds(2, 2)], wg.at[yl, pl.ds(2, 2)], wy_send.at[1], wy_recv.at[1], down),
    ]
    for copy in wy:
        copy.start()

    def s3_copy(j):
        slot = lax.rem(j - yh + 4, 4)
        return remote(s3s.at[j], s3r.at[slot], s3_send.at[j], s3_recv.at[slot], at(z, x, 2 * j + yl, c))

    for j in range(HEADS):
        for copy in s2[j]:
            copy.wait_recv()
        total = qs[j, :, x].reshape(160, 128)
        for d in range(NX - 1):
            total += s2r[j, d].astype(F32)
        rs[j] = total
        s3s[j] = total.astype(BF16)

        @pl.when(j != yh)
        def _(j=j):
            s3_copy(j).start()

    for slot in range(1, 4):
        remote(s3s.at[0], s3r.at[slot], s3_send.at[0], s3_recv.at[slot], sibling).wait_recv()
    total = rs[yh]
    for slot in range(1, 4):
        total += s3r[slot].astype(F32)
    total = total.reshape(4, ROWS, 128)
    zo[...] = total
    zs[...] = jnp.concatenate([total, jnp.zeros((4, 8, 128), F32)], 1).astype(BF16)

    def z_copy(i):
        other = 4 * c + i
        slot = lax.rem(other - z + NZ, NZ)
        return remote(zs.at[i], zr.at[slot], z_send.at[i], z_recv.at[slot], at(other, x, y, c))

    for i in range(4):
        @pl.when(4 * c + i != z)
        def _(i=i):
            z_copy(i).start()

    remote(wg.at[yl, pl.ds(0, 2)], wg.at[1 - yl, pl.ds(0, 2)], wy_send.at[0], wy_recv.at[0], up).wait_recv()
    remote(wg.at[yl, pl.ds(2, 2)], wg.at[1 - yl, pl.ds(2, 2)], wy_send.at[1], wy_recv.at[1], down).wait_recv()
    for b in range(16):
        even = wg[0, b % 4, b // 4].astype(F32)
        odd = wg[1, b % 4, b // 4].astype(F32)
        for p in range(4):
            part = slice(p * ROWS, (p + 1) * ROWS)
            wf[b * 80:(b + 1) * 80, p * 128:(p + 1) * 128] = jnp.concatenate([even[part], odd[part]], 0).astype(BF16)
    for b in range(5):
        cols = slice(b * 256, (b + 1) * 256)
        gs[:, cols] = lax.dot_general(vg[1], wf[cols, :], NT, preferred_element_type=F32).astype(BF16)
    mine = gi_ref.at[:, pl.ds(pl.multiple_of(c * HALF, 128), HALF)]
    theirs = gi_ref.at[:, pl.ds(pl.multiple_of((1 - c) * HALF, 128), HALF)]
    give = remote(gs, mine, gs_send, gs_recv, sibling)
    take = remote(gs, theirs, gs_send, gs_recv, sibling)
    give.start()
    for b in range(5):
        cols = slice(b * 256, (b + 1) * 256)
        go[:, cols] = lax.dot_general(vg[0], wf[cols, :], NT, preferred_element_type=F32).astype(BF16)
    keep = pltpu.make_async_copy(go, mine, go_sem)
    keep.start()

    share = remote(fs, fr, f_send, f_recv, sibling)

    @pl.when(c == zc)
    def _():
        for slot in range(1, NZ):
            remote(zs.at[0], zr.at[slot], z_send.at[0], z_recv.at[slot], sibling).wait_recv()
        total = zo[zi]
        for slot in range(1, NZ):
            total += zr[slot].astype(F32)[:ROWS]
        turned = pltpu.roll(total, 64, 1)
        fs[...] = jnp.where(c == 0, turned, total)
        share.start()
        gw_ref[...] = jnp.where(c == 0, total, turned)[:, :64]
        share.wait_send()

    @pl.when(c != zc)
    def _():
        share.wait_recv()
        gw_ref[...] = fr[:, :64]

    for copy in reward_copies + [share_u, share_h] + wx + wy:
        copy.wait_send()
    for copies in s1 + s2:
        for copy in copies:
            copy.wait_send()
    for i in range(4):
        @pl.when(4 * c + i != z)
        def _(i=i):
            w_send(i).wait_send()
            z_copy(i).wait_send()

        @pl.when(i != yh)
        def _(i=i):
            s3_copy(i).wait_send()
    keep.wait()
    give.wait_send()
    take.wait_recv()


def local(hidden_in, queries, keys, logp_grad, lengths, rewards, w_value):
    vmem = pltpu.VMEM
    dma = pltpu.SemaphoreType.DMA
    anywhere = pl.BlockSpec(memory_space=pl.ANY)
    scalar = pl.BlockSpec(memory_space=pltpu.SMEM)
    gradient, input_grad = pl.pallas_call(
        kernel,
        out_shape=(
            jax.ShapeDtypeStruct((ROWS, 64), F32),
            jax.ShapeDtypeStruct((LEN, FEATURES), BF16),
        ),
        in_specs=[anywhere] * 4 + [scalar] * 2 + [anywhere],
        out_specs=(pl.BlockSpec(memory_space=pltpu.VMEM), anywhere),
        scratch_shapes=[
            vmem((HEADS, LEN, RATIO * WIDTH), BF16),
            vmem((HEADS, LEN, WIDTH), BF16),
            vmem((HEADS, LEN, RATIO * WIDTH), BF16),
            vmem((2, LEN, HALF), BF16),
            vmem((ROWS, 512), BF16),
            vmem((2, HALF, LEN), BF16),
            vmem((2, HEADS, LEN, WIDTH), BF16),
            vmem((2, LEN, 512), BF16),
            vmem((8, 128), F32),
            vmem((MEMBERS, 8, 128), F32),
            vmem((HEADS, 16, 2, ROWS, 128), F32),
            vmem((HEADS, 640, 128), BF16),
            vmem((HEADS, 640, 128), BF16),
            vmem((HEADS, 4, NX, ROWS, 128), F32),
            vmem((HEADS, 3, 160, 128), BF16),
            vmem((HEADS, 3, 160, 128), BF16),
            vmem((HEADS, 160, 128), F32),
            vmem((HEADS, 160, 128), BF16),
            vmem((4, 160, 128), BF16),
            vmem((4, ROWS, 128), F32),
            vmem((4, 48, 128), BF16),
            vmem((NZ, 48, 128), BF16),
            vmem((ROWS, 128), F32),
            vmem((ROWS, 128), F32),
            vmem((160, 128), BF16),
            vmem((2, NX, 4, 160, 128), BF16),
            vmem((HALF, 512), BF16),
            vmem((LEN, HALF), BF16),
            vmem((LEN, HALF), BF16),
            dma((14,)),
            dma((2,)), dma((2,)),
            dma((MEMBERS,)), dma((MEMBERS,)),
            dma((HEADS, 2)), dma((HEADS, 2)),
            dma((HEADS, 3)), dma((HEADS, 3)),
            dma((HEADS,)), dma((4,)),
            dma((4,)), dma((NZ,)),
            dma, dma,
            dma((4,)), dma((4,)),
            dma((3,)), dma((3,)),
            dma((2,)), dma((2,)),
            dma, dma, dma,
        ],
        compiler_params=pltpu.CompilerParams(
            collective_id=0, has_side_effects=True, vmem_limit_bytes=56 * 2 ** 20
        ),
    )(
        hidden_in.reshape(LEN, FEATURES), queries.reshape(LEN, FEATURES), keys.reshape(LEN, 512),
        logp_grad.reshape(LEN, FEATURES), lengths, rewards, w_value,
    )
    return gradient, input_grad.reshape(1, 1, LEN, FEATURES)


def solution(mesh):
    placed = (
        P("fsdp", "grp", None, None),
        P("fsdp", "grp", None, None),
        P("fsdp", "grp", None, None),
        P("fsdp", "grp", None, None),
        P("fsdp", "grp"),
        P("fsdp", "grp"),
        P("fsdp", None),
    )
    return jax.shard_map(
        local,
        mesh=mesh,
        in_specs=placed,
        out_specs=(P("fsdp", "grp"), P("fsdp", "grp", None, None)),
        check_vma=False,
    )
```

```python
import jax
import jax.numpy as jnp
from jax import lax
from jax.experimental import pallas as pl
from jax.experimental.pallas import tpu as pltpu
from jax.sharding import PartitionSpec as P

F32 = jnp.float32
BF16 = jnp.bfloat16
MESH = pl.DeviceIdType.MESH

HEADS = 4
RATIO = 5
WIDTH = 128
LEN = 224
FEATURES = 2560
HALF = 1280
ROWS = 40
MEMBERS = 8
NX, NY, NZ = 4, 8, 8
SPLIT = 112
EXPONENT_SCALE = 1.4426950408889634 * WIDTH ** -0.5
NT = (((1,), (1,)), ((), ()))


def softmax_columns(scores, weight):
    top = jnp.max(scores, axis=0, keepdims=True)
    grown = jnp.exp2((scores - top) * EXPONENT_SCALE)
    total = jnp.sum(grown, axis=0, keepdims=True)
    return (grown * (weight / total)).astype(BF16)


def head_gradient(keys, queries, cotangent, alive):
    upper = lax.broadcasted_iota(jnp.int32, (128, 128), 0) <= lax.broadcasted_iota(jnp.int32, (128, 128), 1)
    corner = lax.broadcasted_iota(jnp.int32, (96, 96), 0) <= lax.broadcasted_iota(jnp.int32, (96, 96), 1)
    total = None
    for h in range(RATIO):
        cols = slice(h * WIDTH, (h + 1) * WIDTH)
        early = lax.dot_general(keys[:128], queries[:128, cols], NT, preferred_element_type=F32)
        late = lax.dot_general(keys, queries[128:, cols], NT, preferred_element_type=F32)
        early = jnp.where(upper, early, -1e30)
        late = jnp.concatenate([late[:128], jnp.where(corner, late[128:], -1e30)], 0)
        early = softmax_columns(early, alive[:, :128])
        late = softmax_columns(late, alive[:, 128:])
        probs = jnp.concatenate(
            [jnp.concatenate([early, jnp.zeros((96, 128), BF16)], 0), late], 1
        )
        part = jnp.dot(probs, cotangent[:, cols], preferred_element_type=F32)
        total = part if total is None else total + part
    return total


def kernel(
    hid, queries, keys, logp, length_ref, reward_ref, w_ref,
    gw_ref, gi_ref,
    qb, kb, gb, hb, wb, ht, ub, vg, rw_src, rw,
    pb, s1s, s1r, qs, s2s, s2r, rs, s3s, s3r, zo, zs, zr, fs, fr,
    ws, wg, wf, gs,
    in_sem, ex_send, ex_recv, rw_send, rw_recv,
    s1_send, s1_recv, s2_send, s2_recv, s3_send, s3_recv, z_send, z_recv, f_send, f_recv,
    wz_send, wz_recv, wx_send, wx_recv, wy_send, wy_recv,
    ry_send, ry_recv, rx_send, rx_recv, rz_send, rz_recv, gs_send, gs_recv,
):
    g = lax.axis_index("grp")
    f = lax.axis_index("fsdp")
    c = lax.rem(g, 2)
    yh = g // 2
    yl = lax.rem(f, 2)
    x = lax.rem(f // 2, NX)
    z = f // (2 * NX)
    zc = z // 4
    zi = lax.rem(z, 4)
    y = 2 * yh + yl

    def at(z_, x_, y_, c_):
        return (2 * (y_ // 2) + c_, (z_ * NX + x_) * 2 + lax.rem(y_, 2))

    sibling = at(z, x, y, 1 - c)
    group = [(lax.rem(g + d, MEMBERS), f) for d in range(1, MEMBERS)]
    up = at(z, x, lax.rem(y + 1, NY), c)
    down = at(z, x, lax.rem(y + NY - 1, NY), c)
    xs = [at(z, lax.rem(x + d, NX), y, c) for d in range(1, NX)]
    zs_both = [at(lax.rem(z + d, NZ), x, y, k) for d in range(1, NZ) for k in range(2)]

    barrier = pltpu.get_barrier_semaphore()
    partners = group + [up, down] + xs + zs_both
    for device in partners:
        pl.semaphore_signal(barrier, inc=1, device_id=device, device_id_type=MESH)

    def remote(src, dst, send, recv, device):
        return pltpu.make_async_remote_copy(
            src_ref=src, dst_ref=dst, send_sem=send, recv_sem=recv, device_id=device, device_id_type=MESH
        )

    loads = []
    for j in range(HEADS):
        wide = pl.ds(j * RATIO * WIDTH, RATIO * WIDTH)
        loads.append([
            pltpu.make_async_copy(keys.at[:, pl.ds(j * WIDTH, WIDTH)], kb.at[j], in_sem.at[3 * j]),
            pltpu.make_async_copy(queries.at[:, wide], qb.at[j], in_sem.at[3 * j + 1]),
            pltpu.make_async_copy(logp.at[:, wide], gb.at[j], in_sem.at[3 * j + 2]),
        ])
    load_w = pltpu.make_async_copy(w_ref, wb, in_sem.at[12])
    load_h = pltpu.make_async_copy(hid.at[:, pl.ds(pl.multiple_of(c * HALF, 128), HALF)], hb.at[0], in_sem.at[13])
    for copy in loads[0] + loads[1] + [load_w] + loads[2] + loads[3] + [load_h]:
        copy.start()

    reward = reward_ref[0, 0].astype(F32)
    length = length_ref[0, 0]
    row = lax.broadcasted_iota(jnp.int32, (8, 128), 0)
    rw_src[...] = jnp.where(row == 0, reward, length.astype(F32))

    alive = jnp.where(lax.broadcasted_iota(jnp.int32, (1, LEN), 1) < length, 1.0, 0.0).astype(F32)

    def attend(j):
        for copy in loads[j]:
            copy.wait()
        ub[0, j] = head_gradient(kb[j], qb[j], gb[j], alive).astype(BF16)

    load_w.wait()
    shard = wb[...].astype(F32)
    ws[...] = jnp.concatenate([shard[:, p * 128:(p + 1) * 128] for p in range(4)], 0).astype(BF16)

    @pl.when(c == zc)
    def _():
        wg[yl, x, zi] = ws[...]

    attend(0)

    pl.semaphore_wait(barrier, len(partners))

    reward_copies = [remote(rw_src, rw.at[d], rw_send.at[d], rw_recv.at[d], group[d - 1]) for d in range(1, MEMBERS)]
    for copy in reward_copies:
        copy.start()
    share_h = remote(
        hid.at[:, pl.ds(pl.multiple_of((1 - c) * HALF, 128), HALF)], hb.at[1], ex_send.at[HEADS], ex_recv.at[HEADS], sibling
    )
    share_h.start()
    share_u = [remote(ub.at[0, j], ub.at[1, j], ex_send.at[j], ex_recv.at[j], sibling) for j in range(HEADS)]
    share_u[0].start()

    first, rest = pl.ds(0, SPLIT), pl.ds(SPLIT, 160 - SPLIT)

    def w_send(i):
        other = 4 * c + i
        return remote(ws.at[first], wg.at[yl, x, zi, first], wz_send.at[i], wz_recv.at[zi], at(other, x, y, zc))

    def w_arrival(i):
        return remote(
            ws.at[first], wg.at[yl, x, i, first], wz_send.at[i], wz_recv.at[i], at(4 * c + i, x, y, zc)
        )

    for i in range(4):
        @pl.when(4 * c + i != z)
        def _(i=i):
            w_send(i).start()

    rest_y = remote(ws.at[rest], wg.at[yl, x, zi, rest], ry_send, ry_recv, up)
    rest_y_arrival = remote(ws.at[rest], wg.at[1 - yl, x, zi, rest], ry_send, ry_recv, up)
    rest_x = [
        remote(wg.at[:, x, zi, rest], wg.at[:, x, zi, rest], rx_send.at[d], rx_recv.at[d], xs[d]) for d in range(NX - 1)
    ]
    rest_x_arrival = [
        remote(
            wg.at[:, x, zi, rest], wg.at[:, lax.rem(x + NX - 1 - d, NX), zi, rest],
            rx_send.at[d], rx_recv.at[d], xs[d],
        )
        for d in range(NX - 1)
    ]
    rest_z = [
        remote(
            wg.at[:, :, zi, rest], wg.at[:, :, zi, rest], rz_send.at[d], rz_recv.at[zi],
            at(lax.rem(z + d + 1, NZ), x, y, c),
        )
        for d in range(NZ - 1)
    ]

    def rest_z_arrival(i):
        return remote(
            wg.at[:, :, i, rest], wg.at[:, :, i, rest], rz_send.at[0], rz_recv.at[i], at(4 * c + i, x, y, c)
        )

    @pl.when(c == zc)
    def _():
        rest_y.start()

    for j in range(1, HEADS):
        attend(j)
        share_u[j].start()

    load_h.wait()
    for b in range(10):
        cols = slice(b * 128, (b + 1) * 128)
        ht[0, cols, :] = hb[0, :, cols].T

    @pl.when(c == zc)
    def _():
        rest_y_arrival.wait_recv()
        for copy in rest_x:
            copy.start()

    share_h.wait_recv()
    for b in range(10):
        cols = slice(b * 128, (b + 1) * 128)
        ht[1, cols, :] = hb[1, :, cols].T
    for copy in share_u:
        copy.wait_recv()

    for copy in reward_copies:
        copy.wait_recv()
    rw[0] = rw_src[...]
    everyone = rw[...]
    rewards = everyone[:, 0:1, :]
    average = jnp.sum(rewards, axis=0) / MEMBERS
    second = jnp.sum(rewards * rewards, axis=0) / MEMBERS
    spread = jnp.maximum(jnp.sqrt(second - average * average), 1.0)

    def factor_of(rows):
        return -((rows[0:1] - average) / spread) / (MEMBERS * rows[1:2])

    own_factor = factor_of(rw_src[...])
    other_factor = factor_of(rw[7 - 6 * c])

    s1 = []
    for j in range(HEADS):
        lanes = slice(j * 128, (j + 1) * 128)
        vg[0, :, lanes] = (ub[0, j].astype(F32) * own_factor).astype(BF16)
        vg[1, :, lanes] = (ub[1, j].astype(F32) * other_factor).astype(BF16)
        for b in range(4):
            rows = slice(b * 320, (b + 1) * 320)
            part = jnp.dot(ht[0, rows, :], vg[0, :, lanes], preferred_element_type=F32)
            part += jnp.dot(ht[1, rows, :], vg[1, :, lanes], preferred_element_type=F32)
            pb[j, b * 4:(b + 1) * 4] = part.reshape(4, 2, ROWS, 128)
        s1s[j] = pb[j, :, 1 - yl].reshape(640, 128).astype(BF16)
        copies = [
            remote(s1s.at[j, pl.ds(0, 320)], s1r.at[j, pl.ds(0, 320)], s1_send.at[j, 0], s1_recv.at[j, 0], up),
            remote(s1s.at[j, pl.ds(320, 320)], s1r.at[j, pl.ds(320, 320)], s1_send.at[j, 1], s1_recv.at[j, 1], down),
        ]
        for copy in copies:
            copy.start()
        s1.append(copies)

    @pl.when(c == zc)
    def _():
        for copy in rest_x_arrival:
            copy.wait_recv()
        for copy in rest_z:
            copy.start()

    for i in range(4):
        @pl.when(4 * c + i != z)
        def _(i=i):
            w_arrival(i).wait_recv()
    ours = wg.at[yl, x, :, first]
    wx = [remote(ours, ours, wx_send.at[d], wx_recv.at[d], xs[d]) for d in range(NX - 1)]
    for copy in wx:
        copy.start()

    s2 = []
    for j in range(HEADS):
        for copy in s1[j]:
            copy.wait_recv()
        qs[j] = (pb[j, :, yl] + s1r[j].astype(F32).reshape(16, ROWS, 128)).reshape(4, 4, ROWS, 128)
        copies = []
        for d in range(NX - 1):
            s2s[j, d] = qs[j, :, lax.rem(x + d + 1, NX)].reshape(160, 128).astype(BF16)
            copies.append(remote(s2s.at[j, d], s2r.at[j, d], s2_send.at[j, d], s2_recv.at[j, d], xs[d]))
            copies[-1].start()
        s2.append(copies)

    def wx_arrival(d):
        return remote(
            ours, wg.at[yl, lax.rem(x + NX - 1 - d, NX), :, first], wx_send.at[d], wx_recv.at[d], xs[d]
        )

    for d in range(NX - 1):
        wx_arrival(d).wait_recv()
    lower, upper = pl.ds(0, 2), pl.ds(2, 2)
    wy = [
        remote(wg.at[yl, lower, :, first], wg.at[yl, lower, :, first], wy_send.at[0], wy_recv.at[0], up),
        remote(wg.at[yl, upper, :, first], wg.at[yl, upper, :, first], wy_send.at[1], wy_recv.at[1], down),
    ]
    wy_arrival = [
        remote(wg.at[yl, lower, :, first], wg.at[1 - yl, lower, :, first], wy_send.at[0], wy_recv.at[0], up),
        remote(wg.at[yl, upper, :, first], wg.at[1 - yl, upper, :, first], wy_send.at[1], wy_recv.at[1], down),
    ]
    for copy in wy:
        copy.start()

    def s3_copy(j):
        slot = lax.rem(j - yh + 4, 4)
        return remote(s3s.at[j], s3r.at[slot], s3_send.at[j], s3_recv.at[slot], at(z, x, 2 * j + yl, c))

    for j in range(HEADS):
        for copy in s2[j]:
            copy.wait_recv()
        total = qs[j, :, x].reshape(160, 128)
        for d in range(NX - 1):
            total += s2r[j, d].astype(F32)
        rs[j] = total
        s3s[j] = total.astype(BF16)

        @pl.when(j != yh)
        def _(j=j):
            s3_copy(j).start()

    for slot in range(1, 4):
        remote(s3s.at[0], s3r.at[slot], s3_send.at[0], s3_recv.at[slot], sibling).wait_recv()
    total = rs[yh]
    for slot in range(1, 4):
        total += s3r[slot].astype(F32)
    total = total.reshape(4, ROWS, 128)
    zo[...] = total
    zs[...] = jnp.concatenate([total, jnp.zeros((4, 8, 128), F32)], 1).astype(BF16)

    def z_copy(i):
        other = 4 * c + i
        slot = lax.rem(other - z + NZ, NZ)
        return remote(zs.at[i], zr.at[slot], z_send.at[i], z_recv.at[slot], at(other, x, y, c))

    for i in range(4):
        @pl.when(4 * c + i != z)
        def _(i=i):
            z_copy(i).start()

    for copy in wy_arrival:
        copy.wait_recv()
    for i in range(4):
        @pl.when(4 * c + i != z)
        def _(i=i):
            rest_z_arrival(i).wait_recv()
    for b in range(16):
        even = wg[0, b % 4, b // 4].astype(F32)
        odd = wg[1, b % 4, b // 4].astype(F32)
        for p in range(4):
            part = slice(p * ROWS, (p + 1) * ROWS)
            wf[b * 80:(b + 1) * 80, p * 128:(p + 1) * 128] = jnp.concatenate([even[part], odd[part]], 0).astype(BF16)
    for b in range(5):
        cols = slice(b * 256, (b + 1) * 256)
        gs[:, cols] = lax.dot_general(vg[1], wf[cols, :], NT, preferred_element_type=F32).astype(BF16)
    give = remote(gs, gi_ref.at[c], gs_send, gs_recv, sibling)
    take = remote(gs, gi_ref.at[1 - c], gs_send, gs_recv, sibling)
    give.start()
    for b in range(5):
        cols = slice(b * 256, (b + 1) * 256)
        gi_ref[c, :, cols] = lax.dot_general(vg[0], wf[cols, :], NT, preferred_element_type=F32).astype(BF16)

    for copy in reward_copies + share_u + [share_h] + wx + wy:
        copy.wait_send()
    for copies in s1 + s2:
        for copy in copies:
            copy.wait_send()

    @pl.when(c == zc)
    def _():
        rest_y.wait_send()
        for copy in rest_x + rest_z:
            copy.wait_send()

    for i in range(4):
        @pl.when(4 * c + i != z)
        def _(i=i):
            w_send(i).wait_send()
            z_copy(i).wait_send()

        @pl.when(i != yh)
        def _(i=i):
            s3_copy(i).wait_send()
    give.wait_send()
    take.wait_recv()

    share = remote(fs, fr, f_send, f_recv, sibling)

    @pl.when(c == zc)
    def _():
        for slot in range(1, NZ):
            remote(zs.at[0], zr.at[slot], z_send.at[0], z_recv.at[slot], sibling).wait_recv()
        total = zo[zi]
        for slot in range(1, NZ):
            total += zr[slot].astype(F32)[:ROWS]
        turned = pltpu.roll(total, 64, 1)
        fs[...] = jnp.where(c == 0, turned, total)
        share.start()
        gw_ref[...] = jnp.where(c == 0, total, turned)[:, :64]
        share.wait_send()

    @pl.when(c != zc)
    def _():
        share.wait_recv()
        gw_ref[...] = fr[:, :64]


def store(gradient, halves, gradient_out, input_out, sem):
    copies = [pltpu.make_async_copy(gradient, gradient_out, sem.at[2])]
    for k in range(2):
        copies.append(pltpu.make_async_copy(halves.at[k], input_out.at[:, pl.ds(k * HALF, HALF)], sem.at[k]))
    for copy in copies:
        copy.start()
    for copy in copies:
        copy.wait()


def local(hidden_in, queries, keys, logp_grad, lengths, rewards, w_value):
    vmem = pltpu.VMEM
    dma = pltpu.SemaphoreType.DMA
    anywhere = pl.BlockSpec(memory_space=pl.ANY)
    scalar = pl.BlockSpec(memory_space=pltpu.SMEM)
    gradient, halves = pl.pallas_call(
        kernel,
        out_shape=(
            vmem((ROWS, 64), F32),
            vmem((2, LEN, HALF), BF16),
        ),
        in_specs=[anywhere] * 4 + [scalar] * 2 + [anywhere],
        out_specs=(pl.BlockSpec(memory_space=pltpu.VMEM),) * 2,
        scratch_shapes=[
            vmem((HEADS, LEN, RATIO * WIDTH), BF16),
            vmem((HEADS, LEN, WIDTH), BF16),
            vmem((HEADS, LEN, RATIO * WIDTH), BF16),
            vmem((2, LEN, HALF), BF16),
            vmem((ROWS, 512), BF16),
            vmem((2, HALF, LEN), BF16),
            vmem((2, HEADS, LEN, WIDTH), BF16),
            vmem((2, LEN, 512), BF16),
            vmem((8, 128), F32),
            vmem((MEMBERS, 8, 128), F32),
            vmem((HEADS, 16, 2, ROWS, 128), F32),
            vmem((HEADS, 640, 128), BF16),
            vmem((HEADS, 640, 128), BF16),
            vmem((HEADS, 4, NX, ROWS, 128), F32),
            vmem((HEADS, 3, 160, 128), BF16),
            vmem((HEADS, 3, 160, 128), BF16),
            vmem((HEADS, 160, 128), F32),
            vmem((HEADS, 160, 128), BF16),
            vmem((4, 160, 128), BF16),
            vmem((4, ROWS, 128), F32),
            vmem((4, 48, 128), BF16),
            vmem((NZ, 48, 128), BF16),
            vmem((ROWS, 128), F32),
            vmem((ROWS, 128), F32),
            vmem((160, 128), BF16),
            vmem((2, NX, 4, 160, 128), BF16),
            vmem((HALF, 512), BF16),
            vmem((LEN, HALF), BF16),
            dma((14,)),
            dma((HEADS + 1,)), dma((HEADS + 1,)),
            dma((MEMBERS,)), dma((MEMBERS,)),
            dma((HEADS, 2)), dma((HEADS, 2)),
            dma((HEADS, 3)), dma((HEADS, 3)),
            dma((HEADS,)), dma((4,)),
            dma((4,)), dma((NZ,)),
            dma, dma,
            dma((4,)), dma((4,)),
            dma((3,)), dma((3,)),
            dma((2,)), dma((2,)),
            dma, dma, dma((3,)), dma((3,)), dma((NZ,)), dma((4,)),
            dma, dma,
        ],
        compiler_params=pltpu.CompilerParams(
            collective_id=0, has_side_effects=True, vmem_limit_bytes=56 * 2 ** 20
        ),
    )(
        hidden_in.reshape(LEN, FEATURES), queries.reshape(LEN, FEATURES), keys.reshape(LEN, 512),
        logp_grad.reshape(LEN, FEATURES), lengths, rewards, w_value,
    )
    gradient, input_grad = pl.pallas_call(
        store,
        out_shape=(
            jax.ShapeDtypeStruct((ROWS, 64), F32),
            jax.ShapeDtypeStruct((LEN, FEATURES), BF16),
        ),
        in_specs=[pl.BlockSpec(memory_space=pltpu.VMEM)] * 2,
        out_specs=(anywhere,) * 2,
        scratch_shapes=[dma((3,))],
        compiler_params=pltpu.CompilerParams(vmem_limit_bytes=4 * 2 ** 20),
    )(gradient, halves)
    return gradient, input_grad.reshape(1, 1, LEN, FEATURES)


def solution(mesh):
    placed = (
        P("fsdp", "grp", None, None),
        P("fsdp", "grp", None, None),
        P("fsdp", "grp", None, None),
        P("fsdp", "grp", None, None),
        P("fsdp", "grp"),
        P("fsdp", "grp"),
        P("fsdp", None),
    )
    return jax.shard_map(
        local,
        mesh=mesh,
        in_specs=placed,
        out_specs=(P("fsdp", "grp"), P("fsdp", "grp", None, None)),
        check_vma=False,
    )
```

```python
import jax
import jax.numpy as jnp
from jax import lax
from jax.experimental import pallas as pl
from jax.experimental.pallas import tpu as pltpu
from jax.sharding import PartitionSpec as P

F32 = jnp.float32
BF16 = jnp.bfloat16
MESH = pl.DeviceIdType.MESH

HEADS = 4
RATIO = 5
WIDTH = 128
LEN = 224
FEATURES = 2560
HALF = 1280
ROWS = 40
MEMBERS = 8
NX, NY, NZ = 4, 8, 8
SPLIT = 96
EXPONENT_SCALE = 1.4426950408889634 * WIDTH ** -0.5
NT = (((1,), (1,)), ((), ()))


def softmax_columns(scores, weight):
    top = jnp.max(scores, axis=0, keepdims=True)
    grown = jnp.exp2((scores - top) * EXPONENT_SCALE)
    total = jnp.sum(grown, axis=0, keepdims=True)
    return (grown * (weight / total)).astype(BF16)


def head_gradient(keys, queries, cotangent, alive):
    upper = lax.broadcasted_iota(jnp.int32, (128, 128), 0) <= lax.broadcasted_iota(jnp.int32, (128, 128), 1)
    corner = lax.broadcasted_iota(jnp.int32, (96, 96), 0) <= lax.broadcasted_iota(jnp.int32, (96, 96), 1)
    total = None
    for h in range(RATIO):
        cols = slice(h * WIDTH, (h + 1) * WIDTH)
        early = lax.dot_general(keys[:128], queries[:128, cols], NT, preferred_element_type=F32)
        late = lax.dot_general(keys, queries[128:, cols], NT, preferred_element_type=F32)
        early = jnp.where(upper, early, -1e30)
        late = jnp.concatenate([late[:128], jnp.where(corner, late[128:], -1e30)], 0)
        early = softmax_columns(early, alive[:, :128])
        late = softmax_columns(late, alive[:, 128:])
        probs = jnp.concatenate(
            [jnp.concatenate([early, jnp.zeros((96, 128), BF16)], 0), late], 1
        )
        part = jnp.dot(probs, cotangent[:, cols], preferred_element_type=F32)
        total = part if total is None else total + part
    return total


def kernel(
    hid, queries, keys, logp, length_ref, reward_ref, w_ref,
    gw_ref, gi_ref,
    qb, kb, gb, hb, wb, ht, ub, vg, rw_src, rw,
    pb, s1s, s1r, qs, s2s, s2r, zo, zs, zr, fs, fr,
    ws, wg, wf, gs,
    in_sem, ex_send, ex_recv, rw_send, rw_recv,
    s1_send, s1_recv, s2_send, s2_recv, z_send, z_recv, f_send, f_recv,
    wz_send, wz_recv, wx_send, wx_recv, wy_send, wy_recv,
    ry_send, ry_recv, rx_send, rx_recv, rz_send, rz_recv, gs_send, gs_recv,
):
    g = lax.axis_index("grp")
    f = lax.axis_index("fsdp")
    c = lax.rem(g, 2)
    yh = g // 2
    yl = lax.rem(f, 2)
    x = lax.rem(f // 2, NX)
    z = f // (2 * NX)
    zc = z // 4
    zi = lax.rem(z, 4)
    y = 2 * yh + yl

    def at(z_, x_, y_, c_):
        return (2 * (y_ // 2) + c_, (z_ * NX + x_) * 2 + lax.rem(y_, 2))

    sibling = at(z, x, y, 1 - c)
    group = [(lax.rem(g + d, MEMBERS), f) for d in range(1, MEMBERS)]
    up = at(z, x, lax.rem(y + 1, NY), c)
    down = at(z, x, lax.rem(y + NY - 1, NY), c)
    xs = [at(z, lax.rem(x + d, NX), y, c) for d in range(1, NX)]
    zs_both = [at(lax.rem(z + d, NZ), x, y, k) for d in range(1, NZ) for k in range(2)]

    barrier = pltpu.get_barrier_semaphore()
    partners = group + [up, down] + xs + zs_both
    for device in partners:
        pl.semaphore_signal(barrier, inc=1, device_id=device, device_id_type=MESH)

    @pl.when(c == zc)
    def _():
        for d in range(1, NZ):
            for e in range(1, 4):
                sender = at(lax.rem(z + d, NZ), x, lax.rem(y + 2 * e, NY), c)
                pl.semaphore_signal(barrier, inc=1, device_id=sender, device_id_type=MESH)

    def remote(src, dst, send, recv, device):
        return pltpu.make_async_remote_copy(
            src_ref=src, dst_ref=dst, send_sem=send, recv_sem=recv, device_id=device, device_id_type=MESH
        )

    loads = []
    for j in range(HEADS):
        wide = pl.ds(j * RATIO * WIDTH, RATIO * WIDTH)
        loads.append([
            pltpu.make_async_copy(keys.at[:, pl.ds(j * WIDTH, WIDTH)], kb.at[j], in_sem.at[3 * j]),
            pltpu.make_async_copy(queries.at[:, wide], qb.at[j], in_sem.at[3 * j + 1]),
            pltpu.make_async_copy(logp.at[:, wide], gb.at[j], in_sem.at[3 * j + 2]),
        ])
    load_w = pltpu.make_async_copy(w_ref, wb, in_sem.at[12])
    load_h = pltpu.make_async_copy(hid.at[:, pl.ds(pl.multiple_of(c * HALF, 128), HALF)], hb.at[0], in_sem.at[13])
    for copy in loads[0] + loads[1] + [load_w] + loads[2] + loads[3] + [load_h]:
        copy.start()

    reward = reward_ref[0, 0].astype(F32)
    length = length_ref[0, 0]
    row = lax.broadcasted_iota(jnp.int32, (8, 128), 0)
    rw_src[...] = jnp.where(row == 0, reward, length.astype(F32))

    alive = jnp.where(lax.broadcasted_iota(jnp.int32, (1, LEN), 1) < length, 1.0, 0.0).astype(F32)

    def attend(j):
        for copy in loads[j]:
            copy.wait()
        ub[0, j] = head_gradient(kb[j], qb[j], gb[j], alive).astype(BF16)

    load_w.wait()
    shard = wb[...].astype(F32)
    ws[...] = jnp.concatenate([shard[:, p * 128:(p + 1) * 128] for p in range(4)], 0).astype(BF16)

    @pl.when(c == zc)
    def _():
        wg[yl, x, zi] = ws[...]

    attend(0)

    pl.semaphore_wait(barrier, len(partners) + jnp.where(c == zc, 9, 12))

    reward_copies = [remote(rw_src, rw.at[d], rw_send.at[d], rw_recv.at[d], group[d - 1]) for d in range(1, MEMBERS)]
    for copy in reward_copies:
        copy.start()
    share_h = remote(
        hid.at[:, pl.ds(pl.multiple_of((1 - c) * HALF, 128), HALF)], hb.at[1], ex_send.at[HEADS], ex_recv.at[HEADS], sibling
    )
    share_h.start()
    share_u = [remote(ub.at[0, j], ub.at[1, j], ex_send.at[j], ex_recv.at[j], sibling) for j in range(HEADS)]
    share_u[0].start()

    first, rest = pl.ds(0, SPLIT), pl.ds(SPLIT, 160 - SPLIT)

    def w_send(i):
        other = 4 * c + i
        return remote(ws.at[first], wg.at[yl, x, zi, first], wz_send.at[i], wz_recv.at[zi], at(other, x, y, zc))

    def w_arrival(i):
        return remote(
            ws.at[first], wg.at[yl, x, i, first], wz_send.at[i], wz_recv.at[i], at(4 * c + i, x, y, zc)
        )

    for i in range(4):
        @pl.when(4 * c + i != z)
        def _(i=i):
            w_send(i).start()

    rest_y = remote(ws.at[rest], wg.at[yl, x, zi, rest], ry_send, ry_recv, up)
    rest_y_arrival = remote(ws.at[rest], wg.at[1 - yl, x, zi, rest], ry_send, ry_recv, up)
    rest_x = [
        remote(wg.at[:, x, zi, rest], wg.at[:, x, zi, rest], rx_send.at[d], rx_recv.at[d], xs[d]) for d in range(NX - 1)
    ]
    rest_x_arrival = [
        remote(
            wg.at[:, x, zi, rest], wg.at[:, lax.rem(x + NX - 1 - d, NX), zi, rest],
            rx_send.at[d], rx_recv.at[d], xs[d],
        )
        for d in range(NX - 1)
    ]
    rest_z = [
        remote(
            wg.at[:, :, zi, rest], wg.at[:, :, zi, rest], rz_send.at[d], rz_recv.at[zi],
            at(lax.rem(z + d + 1, NZ), x, y, c),
        )
        for d in range(NZ - 1)
    ]

    def rest_z_arrival(i):
        return remote(
            wg.at[:, :, i, rest], wg.at[:, :, i, rest], rz_send.at[0], rz_recv.at[i], at(4 * c + i, x, y, c)
        )

    @pl.when(c == zc)
    def _():
        rest_y.start()

    for j in range(1, HEADS):
        attend(j)
        share_u[j].start()

    load_h.wait()
    for b in range(10):
        cols = slice(b * 128, (b + 1) * 128)
        ht[0, cols, :] = hb[0, :, cols].T

    @pl.when(c == zc)
    def _():
        rest_y_arrival.wait_recv()
        for copy in rest_x:
            copy.start()

    share_h.wait_recv()
    for b in range(10):
        cols = slice(b * 128, (b + 1) * 128)
        ht[1, cols, :] = hb[1, :, cols].T
    for copy in share_u:
        copy.wait_recv()

    for copy in reward_copies:
        copy.wait_recv()
    rw[0] = rw_src[...]
    everyone = rw[...]
    rewards = everyone[:, 0:1, :]
    average = jnp.sum(rewards, axis=0) / MEMBERS
    second = jnp.sum(rewards * rewards, axis=0) / MEMBERS
    spread = jnp.maximum(jnp.sqrt(second - average * average), 1.0)

    def factor_of(rows):
        return -((rows[0:1] - average) / spread) / (MEMBERS * rows[1:2])

    own_factor = factor_of(rw_src[...])
    other_factor = factor_of(rw[7 - 6 * c])

    s1 = []
    for j in range(HEADS):
        lanes = slice(j * 128, (j + 1) * 128)
        vg[0, :, lanes] = (ub[0, j].astype(F32) * own_factor).astype(BF16)
        vg[1, :, lanes] = (ub[1, j].astype(F32) * other_factor).astype(BF16)
        for b in range(4):
            rows = slice(b * 320, (b + 1) * 320)
            part = jnp.dot(ht[0, rows, :], vg[0, :, lanes], preferred_element_type=F32)
            part += jnp.dot(ht[1, rows, :], vg[1, :, lanes], preferred_element_type=F32)
            pb[j, b * 4:(b + 1) * 4] = part.reshape(4, 2, ROWS, 128)
        s1s[j] = pb[j, :, 1 - yl].reshape(640, 128).astype(BF16)
        copies = [
            remote(s1s.at[j, pl.ds(0, 320)], s1r.at[j, pl.ds(0, 320)], s1_send.at[j, 0], s1_recv.at[j, 0], up),
            remote(s1s.at[j, pl.ds(320, 320)], s1r.at[j, pl.ds(320, 320)], s1_send.at[j, 1], s1_recv.at[j, 1], down),
        ]
        for copy in copies:
            copy.start()
        s1.append(copies)

    @pl.when(c == zc)
    def _():
        for copy in rest_x_arrival:
            copy.wait_recv()
        for copy in rest_z:
            copy.start()

    for i in range(4):
        @pl.when(4 * c + i != z)
        def _(i=i):
            w_arrival(i).wait_recv()
    ours = wg.at[yl, x, :, first]
    wx = [remote(ours, ours, wx_send.at[d], wx_recv.at[d], xs[d]) for d in range(NX - 1)]
    for copy in wx:
        copy.start()

    s2 = []
    for j in range(HEADS):
        for copy in s1[j]:
            copy.wait_recv()
        qs[j] = (pb[j, :, yl] + s1r[j].astype(F32).reshape(16, ROWS, 128)).reshape(4, 4, ROWS, 128)
        copies = []
        for d in range(NX - 1):
            s2s[j, d] = qs[j, :, lax.rem(x + d + 1, NX)].reshape(160, 128).astype(BF16)
            copies.append(remote(s2s.at[j, d], s2r.at[j, d], s2_send.at[j, d], s2_recv.at[j, d], xs[d]))
            copies[-1].start()
        s2.append(copies)

    def wx_arrival(d):
        return remote(
            ours, wg.at[yl, lax.rem(x + NX - 1 - d, NX), :, first], wx_send.at[d], wx_recv.at[d], xs[d]
        )

    for d in range(NX - 1):
        wx_arrival(d).wait_recv()
    lower, upper = pl.ds(0, 2), pl.ds(2, 2)
    wy = [
        remote(wg.at[yl, lower, :, first], wg.at[yl, lower, :, first], wy_send.at[0], wy_recv.at[0], up),
        remote(wg.at[yl, upper, :, first], wg.at[yl, upper, :, first], wy_send.at[1], wy_recv.at[1], down),
    ]
    wy_arrival = [
        remote(wg.at[yl, lower, :, first], wg.at[1 - yl, lower, :, first], wy_send.at[0], wy_recv.at[0], up),
        remote(wg.at[yl, upper, :, first], wg.at[1 - yl, upper, :, first], wy_send.at[1], wy_recv.at[1], down),
    ]
    for copy in wy:
        copy.start()

    def z_slot(j, i):
        return lax.rem(4 * c + i - z + NZ, NZ) * 4 + lax.rem(j - yh + 4, 4)

    def z_copy(j, i):
        slot = z_slot(j, i)
        return remote(
            zs.at[j, i], zr.at[slot], z_send.at[j, i], z_recv.at[slot], at(4 * c + i, x, 2 * j + yl, c)
        )

    for j in range(HEADS):
        for copy in s2[j]:
            copy.wait_recv()
        total = qs[j, :, x].reshape(160, 128)
        for d in range(NX - 1):
            total += s2r[j, d].astype(F32)
        total = total.reshape(4, ROWS, 128)
        zo[j] = total
        zs[j] = jnp.concatenate([total, jnp.zeros((4, 8, 128), F32)], 1).astype(BF16)
        for i in range(4):
            @pl.when(z_slot(j, i) != 0)
            def _(j=j, i=i):
                z_copy(j, i).start()

    for copy in wy_arrival:
        copy.wait_recv()
    for i in range(4):
        @pl.when(4 * c + i != z)
        def _(i=i):
            rest_z_arrival(i).wait_recv()
    for b in range(16):
        even = wg[0, b % 4, b // 4].astype(F32)
        odd = wg[1, b % 4, b // 4].astype(F32)
        for p in range(4):
            part = slice(p * ROWS, (p + 1) * ROWS)
            wf[b * 80:(b + 1) * 80, p * 128:(p + 1) * 128] = jnp.concatenate([even[part], odd[part]], 0).astype(BF16)
    for b in range(5):
        cols = slice(b * 256, (b + 1) * 256)
        gs[:, cols] = lax.dot_general(vg[1], wf[cols, :], NT, preferred_element_type=F32).astype(BF16)
    give = remote(gs, gi_ref.at[c], gs_send, gs_recv, sibling)
    take = remote(gs, gi_ref.at[1 - c], gs_send, gs_recv, sibling)
    give.start()
    for b in range(5):
        cols = slice(b * 256, (b + 1) * 256)
        gi_ref[c, :, cols] = lax.dot_general(vg[0], wf[cols, :], NT, preferred_element_type=F32).astype(BF16)

    for copy in reward_copies + share_u + [share_h] + wx + wy:
        copy.wait_send()
    for copies in s1 + s2:
        for copy in copies:
            copy.wait_send()

    @pl.when(c == zc)
    def _():
        rest_y.wait_send()
        for copy in rest_x + rest_z:
            copy.wait_send()

    for i in range(4):
        @pl.when(4 * c + i != z)
        def _(i=i):
            w_send(i).wait_send()

        for j in range(HEADS):
            @pl.when(z_slot(j, i) != 0)
            def _(i=i, j=j):
                z_copy(j, i).wait_send()
    give.wait_send()
    take.wait_recv()

    share = remote(fs, fr, f_send, f_recv, sibling)

    @pl.when(c == zc)
    def _():
        for slot in range(1, 4 * NZ):
            remote(zs.at[0, 0], zr.at[slot], z_send.at[0, 0], z_recv.at[slot], sibling).wait_recv()
        total = zo[yh, zi]
        for slot in range(1, 4 * NZ):
            total += zr[slot].astype(F32)[:ROWS]
        turned = pltpu.roll(total, 64, 1)
        fs[...] = jnp.where(c == 0, turned, total)
        share.start()
        gw_ref[...] = jnp.where(c == 0, total, turned)[:, :64]
        share.wait_send()

    @pl.when(c != zc)
    def _():
        share.wait_recv()
        gw_ref[...] = fr[:, :64]


def store(gradient, halves, gradient_out, input_out, sem):
    copies = [pltpu.make_async_copy(gradient, gradient_out, sem.at[2])]
    for k in range(2):
        copies.append(pltpu.make_async_copy(halves.at[k], input_out.at[:, pl.ds(k * HALF, HALF)], sem.at[k]))
    for copy in copies:
        copy.start()
    for copy in copies:
        copy.wait()


def local(hidden_in, queries, keys, logp_grad, lengths, rewards, w_value):
    vmem = pltpu.VMEM
    dma = pltpu.SemaphoreType.DMA
    anywhere = pl.BlockSpec(memory_space=pl.ANY)
    scalar = pl.BlockSpec(memory_space=pltpu.SMEM)
    gradient, halves = pl.pallas_call(
        kernel,
        out_shape=(
            vmem((ROWS, 64), F32),
            vmem((2, LEN, HALF), BF16),
        ),
        in_specs=[anywhere] * 4 + [scalar] * 2 + [anywhere],
        out_specs=(pl.BlockSpec(memory_space=pltpu.VMEM),) * 2,
        scratch_shapes=[
            vmem((HEADS, LEN, RATIO * WIDTH), BF16),
            vmem((HEADS, LEN, WIDTH), BF16),
            vmem((HEADS, LEN, RATIO * WIDTH), BF16),
            vmem((2, LEN, HALF), BF16),
            vmem((ROWS, 512), BF16),
            vmem((2, HALF, LEN), BF16),
            vmem((2, HEADS, LEN, WIDTH), BF16),
            vmem((2, LEN, 512), BF16),
            vmem((8, 128), F32),
            vmem((MEMBERS, 8, 128), F32),
            vmem((HEADS, 16, 2, ROWS, 128), F32),
            vmem((HEADS, 640, 128), BF16),
            vmem((HEADS, 640, 128), BF16),
            vmem((HEADS, 4, NX, ROWS, 128), F32),
            vmem((HEADS, 3, 160, 128), BF16),
            vmem((HEADS, 3, 160, 128), BF16),
            vmem((HEADS, 4, ROWS, 128), F32),
            vmem((HEADS, 4, 48, 128), BF16),
            vmem((4 * NZ, 48, 128), BF16),
            vmem((ROWS, 128), F32),
            vmem((ROWS, 128), F32),
            vmem((160, 128), BF16),
            vmem((2, NX, 4, 160, 128), BF16),
            vmem((HALF, 512), BF16),
            vmem((LEN, HALF), BF16),
            dma((14,)),
            dma((HEADS + 1,)), dma((HEADS + 1,)),
            dma((MEMBERS,)), dma((MEMBERS,)),
            dma((HEADS, 2)), dma((HEADS, 2)),
            dma((HEADS, 3)), dma((HEADS, 3)),
            dma((HEADS, 4)), dma((4 * NZ,)),
            dma, dma,
            dma((4,)), dma((4,)),
            dma((3,)), dma((3,)),
            dma((2,)), dma((2,)),
            dma, dma, dma((3,)), dma((3,)), dma((NZ,)), dma((4,)),
            dma, dma,
        ],
        compiler_params=pltpu.CompilerParams(
            collective_id=0, has_side_effects=True, vmem_limit_bytes=56 * 2 ** 20
        ),
    )(
        hidden_in.reshape(LEN, FEATURES), queries.reshape(LEN, FEATURES), keys.reshape(LEN, 512),
        logp_grad.reshape(LEN, FEATURES), lengths, rewards, w_value,
    )
    gradient, input_grad = pl.pallas_call(
        store,
        out_shape=(
            jax.ShapeDtypeStruct((ROWS, 64), F32),
            jax.ShapeDtypeStruct((LEN, FEATURES), BF16),
        ),
        in_specs=[pl.BlockSpec(memory_space=pltpu.VMEM)] * 2,
        out_specs=(anywhere,) * 2,
        scratch_shapes=[dma((3,))],
        compiler_params=pltpu.CompilerParams(vmem_limit_bytes=4 * 2 ** 20),
    )(gradient, halves)
    return gradient, input_grad.reshape(1, 1, LEN, FEATURES)


def solution(mesh):
    placed = (
        P("fsdp", "grp", None, None),
        P("fsdp", "grp", None, None),
        P("fsdp", "grp", None, None),
        P("fsdp", "grp", None, None),
        P("fsdp", "grp"),
        P("fsdp", "grp"),
        P("fsdp", None),
    )
    return jax.shard_map(
        local,
        mesh=mesh,
        in_specs=placed,
        out_specs=(P("fsdp", "grp"), P("fsdp", "grp", None, None)),
        check_vma=False,
    )
```

```python
import jax
import jax.numpy as jnp
from jax import lax
from jax.experimental import pallas as pl
from jax.experimental.pallas import tpu as pltpu
from jax.sharding import PartitionSpec as P

F32 = jnp.float32
BF16 = jnp.bfloat16
MESH = pl.DeviceIdType.MESH

HEADS = 4
RATIO = 5
WIDTH = 128
LEN = 224
FEATURES = 2560
HALF = 1280
ROWS = 40
MEMBERS = 8
NX, NY, NZ = 4, 8, 8
SPLIT = 96
EXPONENT_SCALE = 1.4426950408889634 * WIDTH ** -0.5
NT = (((1,), (1,)), ((), ()))


def softmax_columns(scores, weight):
    top = jnp.max(scores, axis=0, keepdims=True)
    grown = jnp.exp2((scores - top) * EXPONENT_SCALE)
    total = jnp.sum(grown, axis=0, keepdims=True)
    return (grown * (weight / total)).astype(BF16)


def head_gradient(keys, queries, cotangent, alive):
    upper = lax.broadcasted_iota(jnp.int32, (128, 128), 0) <= lax.broadcasted_iota(jnp.int32, (128, 128), 1)
    corner = lax.broadcasted_iota(jnp.int32, (96, 96), 0) <= lax.broadcasted_iota(jnp.int32, (96, 96), 1)
    total = None
    for h in range(RATIO):
        cols = slice(h * WIDTH, (h + 1) * WIDTH)
        early = lax.dot_general(keys[:128], queries[:128, cols], NT, preferred_element_type=F32)
        late = lax.dot_general(keys, queries[128:, cols], NT, preferred_element_type=F32)
        early = jnp.where(upper, early, -1e30)
        late = jnp.concatenate([late[:128], jnp.where(corner, late[128:], -1e30)], 0)
        early = softmax_columns(early, alive[:, :128])
        late = softmax_columns(late, alive[:, 128:])
        probs = jnp.concatenate(
            [jnp.concatenate([early, jnp.zeros((96, 128), BF16)], 0), late], 1
        )
        part = jnp.dot(probs, cotangent[:, cols], preferred_element_type=F32)
        total = part if total is None else total + part
    return total


def kernel(
    hid, queries, keys, logp, length_ref, reward_ref, w_ref,
    gw_ref, gi_ref,
    qb, kb, gb, hb, wb, ht, ub, vg, rw_src, rw,
    pb, s1s, s1r, qs, s2s, s2r, zo, zs, zr, fs, fr,
    ws, wg, wf, gs,
    in_sem, ex_send, ex_recv, rw_send, rw_recv,
    s1_send, s1_recv, s2_send, s2_recv, z_send, z_recv, f_send, f_recv,
    wz_send, wz_recv, wx_send, wx_recv, wy_send, wy_recv,
    ro_send, ro_recv, rz_send, rz_recv, gs_send, gs_recv,
):
    g = lax.axis_index("grp")
    f = lax.axis_index("fsdp")
    c = lax.rem(g, 2)
    yh = g // 2
    yl = lax.rem(f, 2)
    x = lax.rem(f // 2, NX)
    z = f // (2 * NX)
    zc = z // 4
    zi = lax.rem(z, 4)
    y = 2 * yh + yl

    def at(z_, x_, y_, c_):
        return (2 * (y_ // 2) + c_, (z_ * NX + x_) * 2 + lax.rem(y_, 2))

    sibling = at(z, x, y, 1 - c)
    group = [(lax.rem(g + d, MEMBERS), f) for d in range(1, MEMBERS)]
    up = at(z, x, lax.rem(y + 1, NY), c)
    down = at(z, x, lax.rem(y + NY - 1, NY), c)
    xs = [at(z, lax.rem(x + d, NX), y, c) for d in range(1, NX)]
    zs_both = [at(lax.rem(z + d, NZ), x, y, k) for d in range(1, NZ) for k in range(2)]

    barrier = pltpu.get_barrier_semaphore()
    below = [at(z, lax.rem(x + d, NX), lax.rem(y + NY - 1, NY), c) for d in range(1, NX)]
    partners = group + [up, down] + xs + zs_both + below
    for device in partners:
        pl.semaphore_signal(barrier, inc=1, device_id=device, device_id_type=MESH)

    @pl.when(c == zc)
    def _():
        for d in range(1, NZ):
            for e in range(1, 4):
                sender = at(lax.rem(z + d, NZ), x, lax.rem(y + 2 * e, NY), c)
                pl.semaphore_signal(barrier, inc=1, device_id=sender, device_id_type=MESH)

    def remote(src, dst, send, recv, device):
        return pltpu.make_async_remote_copy(
            src_ref=src, dst_ref=dst, send_sem=send, recv_sem=recv, device_id=device, device_id_type=MESH
        )

    loads = []
    for j in range(HEADS):
        wide = pl.ds(j * RATIO * WIDTH, RATIO * WIDTH)
        loads.append([
            pltpu.make_async_copy(keys.at[:, pl.ds(j * WIDTH, WIDTH)], kb.at[j], in_sem.at[3 * j]),
            pltpu.make_async_copy(queries.at[:, wide], qb.at[j], in_sem.at[3 * j + 1]),
            pltpu.make_async_copy(logp.at[:, wide], gb.at[j], in_sem.at[3 * j + 2]),
        ])
    load_w = pltpu.make_async_copy(w_ref, wb, in_sem.at[12])
    load_h = pltpu.make_async_copy(hid.at[:, pl.ds(pl.multiple_of(c * HALF, 128), HALF)], hb.at[0], in_sem.at[13])
    for copy in loads[0] + loads[1] + [load_w] + loads[2] + loads[3] + [load_h]:
        copy.start()

    reward = reward_ref[0, 0].astype(F32)
    length = length_ref[0, 0]
    row = lax.broadcasted_iota(jnp.int32, (8, 128), 0)
    rw_src[...] = jnp.where(row == 0, reward, length.astype(F32))

    alive = jnp.where(lax.broadcasted_iota(jnp.int32, (1, LEN), 1) < length, 1.0, 0.0).astype(F32)

    def attend(j):
        for copy in loads[j]:
            copy.wait()
        ub[0, j] = head_gradient(kb[j], qb[j], gb[j], alive).astype(BF16)

    load_w.wait()
    shard = wb[...].astype(F32)
    ws[...] = jnp.concatenate([shard[:, p * 128:(p + 1) * 128] for p in range(4)], 0).astype(BF16)

    @pl.when(c == zc)
    def _():
        wg[yl, x, zi] = ws[...]

    attend(0)

    pl.semaphore_wait(barrier, len(partners) + jnp.where(c == zc, 9, 12))

    reward_copies = [remote(rw_src, rw.at[d], rw_send.at[d], rw_recv.at[d], group[d - 1]) for d in range(1, MEMBERS)]
    for copy in reward_copies:
        copy.start()
    share_h = remote(
        hid.at[:, pl.ds(pl.multiple_of((1 - c) * HALF, 128), HALF)], hb.at[1], ex_send.at[HEADS], ex_recv.at[HEADS], sibling
    )
    share_h.start()
    share_u = [remote(ub.at[0, j], ub.at[1, j], ex_send.at[j], ex_recv.at[j], sibling) for j in range(HEADS)]
    share_u[0].start()

    first, rest = pl.ds(0, SPLIT), pl.ds(SPLIT, 160 - SPLIT)

    def w_send(i):
        other = 4 * c + i
        return remote(ws.at[first], wg.at[yl, x, zi, first], wz_send.at[i], wz_recv.at[zi], at(other, x, y, zc))

    def w_arrival(i):
        return remote(
            ws.at[first], wg.at[yl, x, i, first], wz_send.at[i], wz_recv.at[i], at(4 * c + i, x, y, zc)
        )

    for i in range(4):
        @pl.when(4 * c + i != z)
        def _(i=i):
            w_send(i).start()

    rest_places = [(lax.rem(x + d, NX), y) for d in range(1, NX)]
    rest_places += [(lax.rem(x + d, NX), lax.rem(y + 1, NY)) for d in range(NX)]
    rest_out = [
        remote(ws.at[rest], wg.at[yl, x, zi, rest], ro_send.at[n], ro_recv.at[yl, x], at(z, to_x, to_y, c))
        for n, (to_x, to_y) in enumerate(rest_places)
    ]
    rest_in = [
        remote(
            ws.at[rest], wg.at[lax.rem(to_y, 2), to_x, zi, rest], ro_send.at[n], ro_recv.at[lax.rem(to_y, 2), to_x],
            sibling,
        )
        for n, (to_x, to_y) in enumerate(rest_places)
    ]
    rest_z = [
        remote(
            wg.at[:, :, zi, rest], wg.at[:, :, zi, rest], rz_send.at[d], rz_recv.at[zi],
            at(lax.rem(z + d + 1, NZ), x, y, c),
        )
        for d in range(NZ - 1)
    ]

    def rest_z_arrival(i):
        return remote(
            wg.at[:, :, i, rest], wg.at[:, :, i, rest], rz_send.at[0], rz_recv.at[i], at(4 * c + i, x, y, c)
        )

    @pl.when(c == zc)
    def _():
        for copy in rest_out:
            copy.start()

    for j in range(1, HEADS):
        attend(j)
        share_u[j].start()

    load_h.wait()
    for b in range(10):
        cols = slice(b * 128, (b + 1) * 128)
        ht[0, cols, :] = hb[0, :, cols].T

    share_h.wait_recv()
    for b in range(10):
        cols = slice(b * 128, (b + 1) * 128)
        ht[1, cols, :] = hb[1, :, cols].T
    for copy in share_u:
        copy.wait_recv()

    for copy in reward_copies:
        copy.wait_recv()
    rw[0] = rw_src[...]
    everyone = rw[...]
    rewards = everyone[:, 0:1, :]
    average = jnp.sum(rewards, axis=0) / MEMBERS
    second = jnp.sum(rewards * rewards, axis=0) / MEMBERS
    spread = jnp.maximum(jnp.sqrt(second - average * average), 1.0)

    def factor_of(rows):
        return -((rows[0:1] - average) / spread) / (MEMBERS * rows[1:2])

    own_factor = factor_of(rw_src[...])
    other_factor = factor_of(rw[7 - 6 * c])

    s1 = []
    for j in range(HEADS):
        lanes = slice(j * 128, (j + 1) * 128)
        vg[0, :, lanes] = (ub[0, j].astype(F32) * own_factor).astype(BF16)
        vg[1, :, lanes] = (ub[1, j].astype(F32) * other_factor).astype(BF16)
        for b in range(4):
            rows = slice(b * 320, (b + 1) * 320)
            part = jnp.dot(ht[0, rows, :], vg[0, :, lanes], preferred_element_type=F32)
            part += jnp.dot(ht[1, rows, :], vg[1, :, lanes], preferred_element_type=F32)
            pb[j, b * 4:(b + 1) * 4] = part.reshape(4, 2, ROWS, 128)
        s1s[j] = pb[j, :, 1 - yl].reshape(640, 128).astype(BF16)
        copies = [
            remote(s1s.at[j, pl.ds(0, 320)], s1r.at[j, pl.ds(0, 320)], s1_send.at[j, 0], s1_recv.at[j, 0], up),
            remote(s1s.at[j, pl.ds(320, 320)], s1r.at[j, pl.ds(320, 320)], s1_send.at[j, 1], s1_recv.at[j, 1], down),
        ]
        for copy in copies:
            copy.start()
        s1.append(copies)
        if j == 0:
            @pl.when(c == zc)
            def _():
                for copy in rest_in:
                    copy.wait_recv()
                for copy in rest_z:
                    copy.start()

    for i in range(4):
        @pl.when(4 * c + i != z)
        def _(i=i):
            w_arrival(i).wait_recv()
    ours = wg.at[yl, x, :, first]
    wx = [remote(ours, ours, wx_send.at[d], wx_recv.at[d], xs[d]) for d in range(NX - 1)]
    for copy in wx:
        copy.start()

    s2 = []
    for j in range(HEADS):
        for copy in s1[j]:
            copy.wait_recv()
        qs[j] = (pb[j, :, yl] + s1r[j].astype(F32).reshape(16, ROWS, 128)).reshape(4, 4, ROWS, 128)
        copies = []
        for d in range(NX - 1):
            s2s[j, d] = qs[j, :, lax.rem(x + d + 1, NX)].reshape(160, 128).astype(BF16)
            copies.append(remote(s2s.at[j, d], s2r.at[j, d], s2_send.at[j, d], s2_recv.at[j, d], xs[d]))
            copies[-1].start()
        s2.append(copies)

    def wx_arrival(d):
        return remote(
            ours, wg.at[yl, lax.rem(x + NX - 1 - d, NX), :, first], wx_send.at[d], wx_recv.at[d], xs[d]
        )

    for d in range(NX - 1):
        wx_arrival(d).wait_recv()
    lower, upper = pl.ds(0, 2), pl.ds(2, 2)
    wy = [
        remote(wg.at[yl, lower, :, first], wg.at[yl, lower, :, first], wy_send.at[0], wy_recv.at[0], up),
        remote(wg.at[yl, upper, :, first], wg.at[yl, upper, :, first], wy_send.at[1], wy_recv.at[1], down),
    ]
    wy_arrival = [
        remote(wg.at[yl, lower, :, first], wg.at[1 - yl, lower, :, first], wy_send.at[0], wy_recv.at[0], up),
        remote(wg.at[yl, upper, :, first], wg.at[1 - yl, upper, :, first], wy_send.at[1], wy_recv.at[1], down),
    ]
    for copy in wy:
        copy.start()

    def z_slot(j, i):
        return lax.rem(4 * c + i - z + NZ, NZ) * 4 + lax.rem(j - yh + 4, 4)

    def z_copy(j, i):
        slot = z_slot(j, i)
        return remote(
            zs.at[j, i], zr.at[slot], z_send.at[j, i], z_recv.at[slot], at(4 * c + i, x, 2 * j + yl, c)
        )

    for j in range(HEADS):
        for copy in s2[j]:
            copy.wait_recv()
        total = qs[j, :, x].reshape(160, 128)
        for d in range(NX - 1):
            total += s2r[j, d].astype(F32)
        total = total.reshape(4, ROWS, 128)
        zo[j] = total
        zs[j] = jnp.concatenate([total, jnp.zeros((4, 8, 128), F32)], 1).astype(BF16)
        for i in range(4):
            @pl.when(z_slot(j, i) != 0)
            def _(j=j, i=i):
                z_copy(j, i).start()

    for copy in wy_arrival:
        copy.wait_recv()
    for i in range(4):
        @pl.when(4 * c + i != z)
        def _(i=i):
            rest_z_arrival(i).wait_recv()
    for b in range(16):
        even = wg[0, b % 4, b // 4].astype(F32)
        odd = wg[1, b % 4, b // 4].astype(F32)
        for p in range(4):
            part = slice(p * ROWS, (p + 1) * ROWS)
            wf[b * 80:(b + 1) * 80, p * 128:(p + 1) * 128] = jnp.concatenate([even[part], odd[part]], 0).astype(BF16)
    for b in range(5):
        cols = slice(b * 256, (b + 1) * 256)
        gs[:, cols] = lax.dot_general(vg[1], wf[cols, :], NT, preferred_element_type=F32).astype(BF16)
    give = remote(gs, gi_ref.at[c], gs_send, gs_recv, sibling)
    take = remote(gs, gi_ref.at[1 - c], gs_send, gs_recv, sibling)
    give.start()
    for b in range(5):
        cols = slice(b * 256, (b + 1) * 256)
        gi_ref[c, :, cols] = lax.dot_general(vg[0], wf[cols, :], NT, preferred_element_type=F32).astype(BF16)

    for copy in reward_copies + share_u + [share_h] + wx + wy:
        copy.wait_send()
    for copies in s1 + s2:
        for copy in copies:
            copy.wait_send()

    @pl.when(c == zc)
    def _():
        for copy in rest_out + rest_z:
            copy.wait_send()

    for i in range(4):
        @pl.when(4 * c + i != z)
        def _(i=i):
            w_send(i).wait_send()

        for j in range(HEADS):
            @pl.when(z_slot(j, i) != 0)
            def _(i=i, j=j):
                z_copy(j, i).wait_send()
    give.wait_send()
    take.wait_recv()

    share = remote(fs, fr, f_send, f_recv, sibling)

    @pl.when(c == zc)
    def _():
        for slot in range(1, 4 * NZ):
            remote(zs.at[0, 0], zr.at[slot], z_send.at[0, 0], z_recv.at[slot], sibling).wait_recv()
        total = zo[yh, zi]
        for slot in range(1, 4 * NZ):
            total += zr[slot].astype(F32)[:ROWS]
        turned = pltpu.roll(total, 64, 1)
        fs[...] = jnp.where(c == 0, turned, total)
        share.start()
        gw_ref[...] = jnp.where(c == 0, total, turned)[:, :64]
        share.wait_send()

    @pl.when(c != zc)
    def _():
        share.wait_recv()
        gw_ref[...] = fr[:, :64]


def store(gradient, halves, gradient_out, input_out, sem):
    copies = [pltpu.make_async_copy(gradient, gradient_out, sem.at[2])]
    for k in range(2):
        copies.append(pltpu.make_async_copy(halves.at[k], input_out.at[:, pl.ds(k * HALF, HALF)], sem.at[k]))
    for copy in copies:
        copy.start()
    for copy in copies:
        copy.wait()


def local(hidden_in, queries, keys, logp_grad, lengths, rewards, w_value):
    vmem = pltpu.VMEM
    dma = pltpu.SemaphoreType.DMA
    anywhere = pl.BlockSpec(memory_space=pl.ANY)
    scalar = pl.BlockSpec(memory_space=pltpu.SMEM)
    gradient, halves = pl.pallas_call(
        kernel,
        out_shape=(
            vmem((ROWS, 64), F32),
            vmem((2, LEN, HALF), BF16),
        ),
        in_specs=[anywhere] * 4 + [scalar] * 2 + [anywhere],
        out_specs=(pl.BlockSpec(memory_space=pltpu.VMEM),) * 2,
        scratch_shapes=[
            vmem((HEADS, LEN, RATIO * WIDTH), BF16),
            vmem((HEADS, LEN, WIDTH), BF16),
            vmem((HEADS, LEN, RATIO * WIDTH), BF16),
            vmem((2, LEN, HALF), BF16),
            vmem((ROWS, 512), BF16),
            vmem((2, HALF, LEN), BF16),
            vmem((2, HEADS, LEN, WIDTH), BF16),
            vmem((2, LEN, 512), BF16),
            vmem((8, 128), F32),
            vmem((MEMBERS, 8, 128), F32),
            vmem((HEADS, 16, 2, ROWS, 128), F32),
            vmem((HEADS, 640, 128), BF16),
            vmem((HEADS, 640, 128), BF16),
            vmem((HEADS, 4, NX, ROWS, 128), F32),
            vmem((HEADS, 3, 160, 128), BF16),
            vmem((HEADS, 3, 160, 128), BF16),
            vmem((HEADS, 4, ROWS, 128), F32),
            vmem((HEADS, 4, 48, 128), BF16),
            vmem((4 * NZ, 48, 128), BF16),
            vmem((ROWS, 128), F32),
            vmem((ROWS, 128), F32),
            vmem((160, 128), BF16),
            vmem((2, NX, 4, 160, 128), BF16),
            vmem((HALF, 512), BF16),
            vmem((LEN, HALF), BF16),
            dma((14,)),
            dma((HEADS + 1,)), dma((HEADS + 1,)),
            dma((MEMBERS,)), dma((MEMBERS,)),
            dma((HEADS, 2)), dma((HEADS, 2)),
            dma((HEADS, 3)), dma((HEADS, 3)),
            dma((HEADS, 4)), dma((4 * NZ,)),
            dma, dma,
            dma((4,)), dma((4,)),
            dma((3,)), dma((3,)),
            dma((2,)), dma((2,)),
            dma((7,)), dma((2, NX)), dma((NZ,)), dma((4,)),
            dma, dma,
        ],
        compiler_params=pltpu.CompilerParams(
            collective_id=0, has_side_effects=True, vmem_limit_bytes=56 * 2 ** 20
        ),
    )(
        hidden_in.reshape(LEN, FEATURES), queries.reshape(LEN, FEATURES), keys.reshape(LEN, 512),
        logp_grad.reshape(LEN, FEATURES), lengths, rewards, w_value,
    )
    gradient, input_grad = pl.pallas_call(
        store,
        out_shape=(
            jax.ShapeDtypeStruct((ROWS, 64), F32),
            jax.ShapeDtypeStruct((LEN, FEATURES), BF16),
        ),
        in_specs=[pl.BlockSpec(memory_space=pltpu.VMEM)] * 2,
        out_specs=(anywhere,) * 2,
        scratch_shapes=[dma((3,))],
        compiler_params=pltpu.CompilerParams(vmem_limit_bytes=4 * 2 ** 20),
    )(gradient, halves)
    return gradient, input_grad.reshape(1, 1, LEN, FEATURES)


def solution(mesh):
    placed = (
        P("fsdp", "grp", None, None),
        P("fsdp", "grp", None, None),
        P("fsdp", "grp", None, None),
        P("fsdp", "grp", None, None),
        P("fsdp", "grp"),
        P("fsdp", "grp"),
        P("fsdp", None),
    )
    return jax.shard_map(
        local,
        mesh=mesh,
        in_specs=placed,
        out_specs=(P("fsdp", "grp"), P("fsdp", "grp", None, None)),
        check_vma=False,
    )
```
